32 devices in a mesh: level: 4 (over z), leaf: 4 (over x, core), rhs: 2 (over y).
Axes of the slice: x: 2, y: 2, z: 4, core: 2. Of those that a mesh axis runs over, the one named last changes fastest.
Arguments:
- charges: float32 [64, 65536], P(None, ('level', 'leaf', 'rhs')), may hold values from -6 to 6
- cluster_order: int32 [65536], P(('level', 'leaf')), may hold values from 0 to 4095, as said below
- near_tiles: float32 [512, 4, 128, 128], P(('level', 'leaf', 'rhs')), may hold values from -0.25 to 0.25
- near_index: int32 [512, 4], P(('level', 'leaf', 'rhs')), may hold values from 0 to 31, as said below
- near_count: int32 [512], P(('level', 'leaf', 'rhs')), may hold values from 1 to 4, as said below
- proj_basis: float32 [4, 65536, 256], P(None, ('level', 'leaf', 'rhs'))
- corr_basis: float32 [4, 256, 65536], P(None, None, ('level', 'leaf', 'rhs')), may hold values from -0.1875 to 0.1875
- coupling: float32 [16, 4, 2, 256, 256], P(('level', 'leaf'))
Outputs:
- solution: float32 [64, 65536], P(None, ('level', 'leaf', 'rhs'))
The draws below stay inside these ranges and needn't reach their ends.
Inputs may be any that keep to these rules, and one draw needn't show every extreme that they name: `cluster_order`: every aligned block of 4096 entries is a permutation of 0 to 4095. `near_index`: the entries of a row are distinct tile numbers of the same leaf, the first being the row's own tile. `near_count`: the first tile row of every leaf has 4.
All inputs are finite; a program needn't handle non-finite values.
Results may differ from the reference program's by a relative error of at most 0.0001.
Values sent between devices are 32-bit elements; how exact they have to be, the bound alone decides.
A program may use at most 128 MiB of HBM per device.

```python
import jax
import jax.numpy as jnp
from jax import lax

RANK = 256
NRHS = 64
TILE = 128
NEAR = 4
LEVELS = 4
LEAF = 4096
NPTS = 65536


def draw_cluster_order(key, part):
    leaves = NPTS // LEAF
    keys = jax.random.split(key, leaves)
    perms = jax.vmap(lambda single: jax.random.permutation(single, LEAF))(keys)
    return perms.reshape(NPTS).astype(jnp.int32)


def draw_near_index(key, part):
    tiles_leaf = LEAF // TILE
    row_total = NPTS // TILE
    keys = jax.random.split(jax.random.fold_in(key, 11), row_total)
    shifts = jax.vmap(lambda single: jax.random.permutation(single, tiles_leaf - 1)[:NEAR - 1] + 1)(keys)
    own_tile = jnp.arange(row_total, dtype=jnp.int32) % tiles_leaf
    offsets = jnp.concatenate([jnp.zeros((row_total, 1), jnp.int32), shifts.astype(jnp.int32)], axis=1)
    return ((own_tile[:, None] + offsets) % tiles_leaf).astype(jnp.int32)


def draw_near_count(key, part):
    tiles_leaf = LEAF // TILE
    row_total = NPTS // TILE
    counts = jax.random.randint(jax.random.fold_in(key, 23), (row_total,), 1, NEAR + 1).astype(jnp.int32)
    first_row = jnp.arange(row_total, dtype=jnp.int32) % tiles_leaf == 0
    return jnp.where(first_row, NEAR, counts).astype(jnp.int32)


def draw_proj_basis(key, part):
    heights = jnp.arange(LEVELS, dtype=jnp.float32)
    scales = (LEAF * 2.0 ** heights) ** (-0.5)
    values = jax.random.normal(key, (LEVELS, NPTS, RANK), jnp.float32)
    return values * scales[:, None, None]


def draw_coupling(key, part):
    leaves = NPTS // LEAF
    shape = (LEVELS, leaves // 2, 2, RANK, 2, RANK)
    noise = jax.random.normal(key, shape, jnp.float32)
    noise = noise * (0.4 / (2.0 * RANK) ** 0.5)
    leaf_ids = jnp.arange(leaves, dtype=jnp.int32)
    eye_block = jnp.eye(RANK, dtype=jnp.float32)
    stacked = []
    for height in range(LEVELS):
        nodes = leaf_ids // 2 ** (height + 1)
        child_bit = leaf_ids // 2 ** height % 2
        blocks = noise[height][nodes]
        first = (child_bit == 0)[:, None, None]
        own_block = jnp.where(first, blocks[:, 1, :, 0, :], blocks[:, 0, :, 1, :])
        sib_block = jnp.where(first, blocks[:, 1, :, 1, :], blocks[:, 0, :, 0, :]) + eye_block[None]
        stacked.append(jnp.stack([own_block, sib_block], axis=1))
    return jnp.stack(stacked, axis=1)


def level_of(key, dims, shards, low, largest):
    factor_of, own = 1.0, jax.random.fold_in(key, 6)
    for position, parts in shards:
        steps = jnp.exp(jax.random.uniform(jax.random.fold_in(own, position), (parts,), jnp.float32, low / len(shards), largest / len(shards)))
        factor_of = factor_of * jnp.repeat(steps, dims[position] // parts).reshape([-1 if axis == position else 1 for axis in range(len(dims))])
    return factor_of


def bell_draw(stream_key, shape, scale, bound, pieces=(), kind=jnp.bfloat16):
    factor_of = level_of(stream_key, shape, pieces, -0.22, 0.18) if pieces else 1.0
    result = jax.random.normal(stream_key, shape, jnp.float32) * scale * factor_of
    return jnp.minimum(jnp.maximum(result, -bound), bound).astype(kind)


def setup_inputs(seed: int = 0) -> dict:
    splits = jax.random.split(jax.random.key(seed), 9)
    charges = bell_draw(splits[0], (NRHS, NPTS), 1.0, 6.0, ((1, 32),), jnp.float32)
    cluster_order = draw_cluster_order(jax.random.fold_in(splits[8], 71), 0)
    near_tiles = bell_draw(splits[2], (NPTS // TILE, NEAR, TILE, TILE), (NEAR * TILE) ** -0.5, 0.25, ((0, 32),), jnp.float32)
    near_index = draw_near_index(jax.random.fold_in(splits[8], 71), 0)
    near_count = draw_near_count(jax.random.fold_in(splits[8], 71), 0)
    proj_basis = draw_proj_basis(jax.random.fold_in(splits[8], 71), 0)
    corr_basis = bell_draw(splits[6], (LEVELS, RANK, NPTS), (4 * RANK) ** -0.5, 0.1875, ((2, 32),), jnp.float32)
    coupling = draw_coupling(jax.random.fold_in(splits[8], 71), 0)
    return {"charges": charges, "cluster_order": cluster_order, "near_tiles": near_tiles, "near_index": near_index, "near_count": near_count, "proj_basis": proj_basis, "corr_basis": corr_basis, "coupling": coupling}


def reference(charges, cluster_order, near_tiles, near_index, near_count, proj_basis, corr_basis, coupling):
    leaves = NPTS // LEAF
    tiles_leaf = LEAF // TILE
    by_leaf = charges.reshape(NRHS, leaves, LEAF)
    local_order = cluster_order.reshape(leaves, LEAF)
    ordered = jnp.take_along_axis(by_leaf, local_order[None, :, :], axis=2)
    blocks = ordered.reshape(NRHS, leaves, tiles_leaf, TILE)
    index = near_index.reshape(leaves, tiles_leaf, NEAR)

    def pick_tiles(leaf_blocks, leaf_index):
        return leaf_blocks[:, leaf_index]

    picked = jax.vmap(pick_tiles, in_axes=(1, 0), out_axes=1)(blocks, index)
    live_mask = (jnp.arange(NEAR)[None, :] < near_count[:, None]).astype(jnp.float32)
    live_mask = live_mask.reshape(leaves, tiles_leaf, NEAR)
    picked = picked * live_mask[None, :, :, :, None]
    tiles = near_tiles.reshape(leaves, tiles_leaf, NEAR, TILE, TILE)
    current = jnp.einsum("rltki,ltkio->rlto", picked, tiles, precision=lax.Precision.HIGHEST)
    current = current.reshape(NRHS, leaves, LEAF)
    for height in range(LEVELS):
        span = 2 ** height
        basis = proj_basis[height].reshape(leaves, LEAF, RANK)
        projected = jnp.einsum("rln,lnk->rlk", current, basis, precision=lax.Precision.HIGHEST)
        own_sum = projected.reshape(NRHS, leaves // span, span, RANK).sum(axis=2)
        sib_sum = jnp.flip(own_sum.reshape(NRHS, leaves // (2 * span), 2, RANK), axis=2)
        sib_sum = sib_sum.reshape(NRHS, leaves // span, RANK)
        own_rows = jnp.repeat(own_sum, span, axis=1)
        sib_rows = jnp.repeat(sib_sum, span, axis=1)
        coeff = jnp.einsum("rlk,lkj->rlj", own_rows, coupling[:, height, 0], precision=lax.Precision.HIGHEST)
        coeff = coeff + jnp.einsum("rlk,lkj->rlj", sib_rows, coupling[:, height, 1], precision=lax.Precision.HIGHEST)
        correction = corr_basis[height].reshape(RANK, leaves, LEAF)
        current = current - jnp.einsum("rlk,kln->rln", coeff, correction, precision=lax.Precision.HIGHEST)
    return current.reshape(NRHS, NPTS)
```

```python
import jax
import jax.numpy as jnp
from jax import lax
from jax.experimental import pallas as pl
from jax.experimental.pallas import tpu as pltpu
from jax.sharding import PartitionSpec as P

F32 = jnp.float32
BF16 = jnp.bfloat16
MESH = pl.DeviceIdType.MESH
POS = 512
SRC = 512
SUB = 256


def flip(index, bit):
    return index + bit - 2 * bit * ((index // bit) % 2)


def split(values):
    high = values.astype(BF16)
    low = (values - high.astype(F32)).astype(BF16)
    return high, low


def stacked(values):
    return jnp.concatenate(split(values), axis=0)


def dot(left, right):
    return jnp.dot(left, right, preferred_element_type=F32)


def dot3(left_hl, right_high, right_low):
    rows = left_hl.shape[0] // 2
    both = dot(left_hl, right_high)
    return both[:rows] + both[rows:] + dot(left_hl[:rows], right_low)


def kernel(
    near_index, near_count, order, charges, near, proj, corr, coup, out,
    mine, other, acc, ordered, near_f, near_hl, proj_f, proj_h, proj_l, corr_f, corr_h, corr_l,
    coup_f, coup_h, coup_l, current, part, rs0, stage0, ag0, rs, stage, ag, zsend, zrecv,
    load_sem, ex_send, ex_recv, rs_send, rs_recv, ag_send, ag_recv, z_send, z_recv,
):
    heights = proj.shape[0]
    rhs_count, half = charges.shape
    level, leaf, side = lax.axis_index("level"), lax.axis_index("leaf"), lax.axis_index("rhs")
    core, column = leaf % 2, leaf // 2
    rank = side + 2 * core + 4 * column
    rank0 = side + 2 * core

    def rank_of(rel):
        number = rank
        for bit in (1, 2, 4):
            if rel & bit:
                number = flip(number, bit)
        return number

    def plane(rel):
        where, there = leaf, side
        if rel & 1:
            there = 1 - side
        if rel & 2:
            where = flip(where, 1)
        if rel & 4:
            where = flip(where, 2)
        return {"level": level, "leaf": where, "rhs": there}

    def column_of(rel):
        number = level
        for bit in (1, 2):
            if rel & bit:
                number = flip(number, bit)
        return {"level": number, "leaf": leaf, "rhs": side}

    loads = [pltpu.make_async_copy(charges, mine, load_sem.at[0])]
    for height in range(heights):
        loads.append(pltpu.make_async_copy(proj.at[height], proj_f.at[height], load_sem.at[1 + 2 * height]))
        loads.append(pltpu.make_async_copy(corr.at[height], corr_f.at[height], load_sem.at[2 + 2 * height]))
    loads.append(pltpu.make_async_copy(near, near_f, load_sem.at[1 + 2 * heights]))
    loads.append(pltpu.make_async_copy(coup, coup_f, load_sem.at[2 + 2 * heights]))
    for load in loads:
        load.start()

    barrier = pltpu.get_barrier_semaphore()
    for rel in range(1, 8):
        pl.semaphore_signal(barrier, inc=1, device_id=plane(rel), device_id_type=MESH)
    for rel in range(1, 4):
        pl.semaphore_signal(barrier, inc=1, device_id=column_of(rel), device_id_type=MESH)
    pl.semaphore_wait(barrier, 10)

    sends = []

    def send(src, dst, send_sem, recv_sem, device):
        copy = pltpu.make_async_remote_copy(
            src_ref=src, dst_ref=dst, send_sem=send_sem, recv_sem=recv_sem,
            device_id=device, device_id_type=MESH,
        )
        copy.start()
        sends.append(copy)
        return copy

    chunks = half // SRC
    arrivals = []
    for chunk in range(chunks):
        cols = pl.ds(chunk * SRC, SRC)
        arrivals.append(send(
            charges.at[:, cols], other.at[:, cols], ex_send.at[chunk], ex_recv.at[chunk], plane(1)
        ))

    rows_of = lax.broadcasted_iota(jnp.int32, (SUB, POS), 0)

    def place(source, first, start, fresh):
        parts = stacked(source[:, pl.ds(start, SRC)])

        def body(step, carry):
            wanted = order[step]
            masks = []
            for sub in range(SRC // SUB):
                rel = wanted - (first + start + sub * SUB)
                masks.append(jnp.where(rows_of == rel, 1.0, 0.0).astype(BF16))
            got = dot(parts, jnp.concatenate(masks, axis=0))
            if fresh:
                acc[step] = got
            else:
                acc[step] = acc[step] + got
            return carry

        lax.fori_loop(0, order.shape[0], body, 0)

    loads[0].wait()
    for chunk in range(chunks):
        place(mine, side * half, chunk * SRC, chunk == 0)

    for height in range(heights):
        loads[1 + 2 * height].wait()
        loads[2 + 2 * height].wait()

        def split_proj(step, carry):
            rows = pl.ds(step * 256, 256)
            high, low = split(proj_f[height, rows, :])
            proj_h[height, rows, :] = high
            proj_l[height, rows, :] = low
            return carry

        def split_corr(step, carry):
            rows = pl.ds(step * 32, 32)
            high, low = split(corr_f[height, rows, :])
            corr_h[height, rows, :] = high
            corr_l[height, rows, :] = low
            return carry

        lax.fori_loop(0, half // 256, split_proj, 0)
        lax.fori_loop(0, corr.shape[1] // 32, split_corr, 0)
    loads[1 + 2 * heights].wait()
    loads[2 + 2 * heights].wait()
    tile_rows, slots, tile = near.shape[0], near.shape[1], near.shape[2]

    def split_near(step, carry):
        for slot in range(slots):
            high, low = split(near_f[step, slot])
            near_hl[step, slot * tile:(slot + 1) * tile, :tile] = high
            near_hl[step, slot * tile:(slot + 1) * tile, tile:] = low
        return carry

    lax.fori_loop(0, tile_rows, split_near, 0)

    def split_coup(step, carry):
        high, low = split(coup_f[step])
        coup_h[step] = high
        coup_l[step] = low
        return carry

    lax.fori_loop(0, heights, split_coup, 0)

    for chunk in range(chunks):
        arrivals[chunk].wait_recv()
        place(other, (1 - side) * half, chunk * SRC, False)

    per = POS // tile

    def cut(step, carry):
        for piece in range(per):
            ordered[step * per + piece] = acc[step, :, piece * tile:(piece + 1) * tile].astype(BF16)
        return carry

    lax.fori_loop(0, order.shape[0], cut, 0)

    for row in range(tile_rows):
        picked = []
        for slot in range(slots):
            live = jnp.where(slot < near_count[row], 1.0, 0.0).astype(F32)
            block = ordered[near_index[row, slot]]
            picked.append((block.astype(F32) * live).astype(BF16))
        four = dot(jnp.concatenate(picked, axis=1), near_hl[row])
        current[:, row * tile:(row + 1) * tile] = (
            four[:rhs_count, :tile] + (four[:rhs_count, tile:] + four[rhs_count:, :tile])
            + four[rhs_count:, tile:]
        )

    for height in range(heights):
        got = dot3(stacked(current[...]), proj_h[height], proj_l[height])
        part[height] = got.reshape(part.shape[1:])
        own = sib = None
        if height == 0:
            waits = []
            for rel in range(1, 4):
                there = rank0
                for bit in (1, 2):
                    if rel & bit:
                        there = flip(there, bit)
                waits.append(send(
                    part.at[0, pl.ds(2 * there, 2)], rs0.at[rel],
                    rs_send.at[0, rel], rs_recv.at[0, rel], plane(rel),
                ))
            for wait in waits:
                wait.wait_recv()
            near_sum = part[0, pl.ds(2 * rank0, 2)] + rs0[1]
            far_sum = rs0[2] + rs0[3]
            stage0[0] = near_sum
            stage0[1] = far_sum
            stage0[2] = near_sum
            ag0[rank0, 0] = near_sum
            ag0[rank0, 1] = far_sum
            waits = []
            for rel in range(1, 4):
                first = 1 if rel & 2 else 0
                waits.append(send(
                    stage0.at[pl.ds(first, 2)], ag0.at[rank0],
                    ag_send.at[0, rel], ag_recv.at[0, rel], plane(rel),
                ))
            for wait in waits:
                wait.wait_recv()
            own = ag0[:, 0].reshape(rhs_count, -1)
            sib = ag0[:, 1].reshape(rhs_count, -1)
        else:
            waits = []
            for rel in range(1, 8):
                waits.append(send(
                    part.at[height, rank_of(rel)], rs.at[height, rel],
                    rs_send.at[height, rel], rs_recv.at[height, rel], plane(rel),
                ))
            for wait in waits:
                wait.wait_recv()
            near_sum = (part[height, rank] + rs[height, 1]) + (rs[height, 2] + rs[height, 3])
            far_sum = (rs[height, 4] + rs[height, 5]) + (rs[height, 6] + rs[height, 7])
            swap = height == 1
            if height > 1:
                whole = near_sum + far_sum
                zsend[height] = whole
                waits = []
                for rel in range(1, 2 ** (height - 1)):
                    waits.append(send(
                        zsend.at[height], zrecv.at[height, rel],
                        z_send.at[height, rel], z_recv.at[height, rel], column_of(rel),
                    ))
                for wait in waits:
                    wait.wait_recv()
                if height == 2:
                    near_sum, far_sum = whole, zrecv[height, 1]
                else:
                    near_sum = whole + zrecv[height, 1]
                    far_sum = zrecv[height, 2] + zrecv[height, 3]
            stage[height, 0] = near_sum
            stage[height, 1] = far_sum
            stage[height, 2] = near_sum
            ag[height, rank, 0] = near_sum
            ag[height, rank, 1] = far_sum
            waits = []
            for rel in range(1, 8):
                first = 1 if swap and rel & 4 else 0
                waits.append(send(
                    stage.at[height, pl.ds(first, 2)], ag.at[height, rank],
                    ag_send.at[height, rel], ag_recv.at[height, rel], plane(rel),
                ))
            for wait in waits:
                wait.wait_recv()
            own = ag[height, :, 0].reshape(rhs_count, -1)
            sib = ag[height, :, 1].reshape(rhs_count, -1)
        coeff = dot3(stacked(own), coup_h[height, 0], coup_l[height, 0])
        coeff = coeff + dot3(stacked(sib), coup_h[height, 1], coup_l[height, 1])
        change = dot3(stacked(coeff), corr_h[height], corr_l[height])
        if height < heights - 1:
            current[...] = current[...] - change
        else:
            out[...] = current[...] - change

    for copy in sends:
        copy.wait_send()


def local(
    charges, cluster_order, near_tiles, near_index, near_count, proj_basis, corr_basis, coupling
):
    rhs_count, half = charges.shape
    heights, _, rank = proj_basis.shape
    leaf_size = cluster_order.shape[0]
    tile_rows, slots, tile, _ = near_tiles.shape
    eighth = rhs_count // 8
    any_space = pl.BlockSpec(memory_space=pl.ANY)
    smem = pl.BlockSpec(memory_space=pltpu.SMEM)
    vmem = pl.BlockSpec(memory_space=pltpu.VMEM)
    dma = pltpu.SemaphoreType.DMA
    return pl.pallas_call(
        kernel,
        out_shape=jax.ShapeDtypeStruct((rhs_count, half), F32),
        in_specs=[smem, smem, vmem, any_space, any_space, any_space, any_space, any_space],
        out_specs=vmem,
        scratch_shapes=[
            pltpu.VMEM((rhs_count, half), F32),
            pltpu.VMEM((rhs_count, half), F32),
            pltpu.VMEM((leaf_size // POS, 2 * rhs_count, POS), F32),
            pltpu.VMEM((leaf_size // tile, 2 * rhs_count, tile), BF16),
            pltpu.VMEM((tile_rows, slots, tile, tile), F32),
            pltpu.VMEM((tile_rows, slots * tile, 2 * tile), BF16),
            pltpu.VMEM((heights, half, rank), F32),
            pltpu.VMEM((heights, half, rank), BF16),
            pltpu.VMEM((heights, half, rank), BF16),
            pltpu.VMEM((heights, rank, half), F32),
            pltpu.VMEM((heights, rank, half), BF16),
            pltpu.VMEM((heights, rank, half), BF16),
            pltpu.VMEM((heights, 2, rank, rank), F32),
            pltpu.VMEM((heights, 2, rank, rank), BF16),
            pltpu.VMEM((heights, 2, rank, rank), BF16),
            pltpu.VMEM((rhs_count, half), F32),
            pltpu.VMEM((heights, 8, eighth, rank), F32),
            pltpu.VMEM((4, 2, eighth, rank), F32),
            pltpu.VMEM((3, 2, eighth, rank), F32),
            pltpu.VMEM((4, 2, 2, eighth, rank), F32),
            pltpu.VMEM((heights, 8, eighth, rank), F32),
            pltpu.VMEM((heights, 3, eighth, rank), F32),
            pltpu.VMEM((heights, 8, 2, eighth, rank), F32),
            pltpu.VMEM((heights, eighth, rank), F32),
            pltpu.VMEM((heights, 4, eighth, rank), F32),
            dma((3 + 2 * heights,)),
            dma((half // SRC,)),
            dma((half // SRC,)),
            dma((heights, 8)),
            dma((heights, 8)),
            dma((heights, 8)),
            dma((heights, 8)),
            dma((heights, 4)),
            dma((heights, 4)),
        ],
        compiler_params=pltpu.CompilerParams(
            collective_id=0, has_side_effects=True, vmem_limit_bytes=60 * 2**20
        ),
        name="solve",
    )(
        near_index,
        near_count,
        cluster_order.reshape(leaf_size // POS, 1, POS),
        charges,
        near_tiles,
        proj_basis,
        corr_basis,
        coupling[0],
    )


def solution(mesh):
    return jax.shard_map(
        local,
        mesh=mesh,
        in_specs=(
            P(None, ("level", "leaf", "rhs")),
            P(("level", "leaf")),
            P(("level", "leaf", "rhs"), None, None, None),
            P(("level", "leaf", "rhs"), None),
            P(("level", "leaf", "rhs")),
            P(None, ("level", "leaf", "rhs"), None),
            P(None, None, ("level", "leaf", "rhs")),
            P(("level", "leaf"), None, None, None, None),
        ),
        out_specs=P(None, ("level", "leaf", "rhs")),
        check_vma=False,
    )
```

```python
import jax
import jax.numpy as jnp
from jax import lax
from jax.experimental import pallas as pl
from jax.experimental.pallas import tpu as pltpu
from jax.sharding import PartitionSpec as P

F32 = jnp.float32
BF16 = jnp.bfloat16
MESH = pl.DeviceIdType.MESH
POS = 512
SRC = 512
SUB = 256


def flip(index, bit):
    return index + bit - 2 * bit * ((index // bit) % 2)


def split(values):
    high = values.astype(BF16)
    low = (values - high.astype(F32)).astype(BF16)
    return high, low


def stacked(values):
    return jnp.concatenate(split(values), axis=0)


def dot(left, right):
    return jnp.dot(left, right, preferred_element_type=F32)


def dot3(left_hl, right_high, right_low):
    rows = left_hl.shape[0] // 2
    both = dot(left_hl, right_high)
    return both[:rows] + both[rows:] + dot(left_hl[:rows], right_low)


def kernel(
    near_index, near_count, order, charges, near, proj, corr, coup, out,
    mine, other, hot, ordered, near_f, near_hl, proj_f, proj_h, proj_l, corr_f, corr_h, corr_l,
    coup_f, coup_h, coup_l, current, part, rs0, stage0, ag0, rs, stage, ag, zsend, zrecv,
    load_sem, ex_send, ex_recv, rs_send, rs_recv, ag_send, ag_recv, z_send, z_recv,
):
    heights = proj.shape[0]
    rhs_count, half = charges.shape
    level, leaf, side = lax.axis_index("level"), lax.axis_index("leaf"), lax.axis_index("rhs")
    core, column = leaf % 2, leaf // 2
    rank = side + 2 * core + 4 * column
    rank0 = side + 2 * core

    def rank_of(rel):
        number = rank
        for bit in (1, 2, 4):
            if rel & bit:
                number = flip(number, bit)
        return number

    def plane(rel):
        where, there = leaf, side
        if rel & 1:
            there = 1 - side
        if rel & 2:
            where = flip(where, 1)
        if rel & 4:
            where = flip(where, 2)
        return {"level": level, "leaf": where, "rhs": there}

    def column_of(rel):
        number = level
        for bit in (1, 2):
            if rel & bit:
                number = flip(number, bit)
        return {"level": number, "leaf": leaf, "rhs": side}

    loads = [pltpu.make_async_copy(charges, mine, load_sem.at[0])]
    for height in range(heights):
        loads.append(pltpu.make_async_copy(proj.at[height], proj_f.at[height], load_sem.at[1 + 2 * height]))
        loads.append(pltpu.make_async_copy(corr.at[height], corr_f.at[height], load_sem.at[2 + 2 * height]))
    loads.append(pltpu.make_async_copy(near, near_f, load_sem.at[1 + 2 * heights]))
    loads.append(pltpu.make_async_copy(coup, coup_f, load_sem.at[2 + 2 * heights]))
    for load in [loads[0], loads[1 + 2 * heights], loads[1], loads[2 + 2 * heights]] + loads[2:1 + 2 * heights]:
        load.start()

    barrier = pltpu.get_barrier_semaphore()
    for rel in range(1, 8):
        pl.semaphore_signal(barrier, inc=1, device_id=plane(rel), device_id_type=MESH)
    for rel in range(1, 4):
        pl.semaphore_signal(barrier, inc=1, device_id=column_of(rel), device_id_type=MESH)
    pl.semaphore_wait(barrier, 10)

    sends = []

    def send(src, dst, send_sem, recv_sem, device):
        copy = pltpu.make_async_remote_copy(
            src_ref=src, dst_ref=dst, send_sem=send_sem, recv_sem=recv_sem,
            device_id=device, device_id_type=MESH,
        )
        copy.start()
        sends.append(copy)
        return copy

    chunks = half // SRC
    arrivals = []
    for chunk in range(chunks):
        cols = pl.ds(chunk * SRC, SRC)
        arrivals.append(send(
            charges.at[:, cols], other.at[:, cols], ex_send.at[chunk], ex_recv.at[chunk], plane(1)
        ))

    rows_of = lax.broadcasted_iota(jnp.int32, (SUB, POS), 0)
    tile_rows, slots, tile = near.shape[0], near.shape[1], near.shape[2]
    per = POS // tile

    def place(source, first, start, width, fresh):
        pieces = width // SUB
        parts = jnp.concatenate(
            [stacked(source[:, start + sub * SUB:start + (sub + 1) * SUB]) for sub in range(pieces)], axis=0
        )
        rows = 2 * rhs_count

        def body(step, carry):
            wanted = order[step]
            if fresh:
                hot[step] = jnp.where(rows_of == wanted % SUB, 1.0, 0.0).astype(BF16)
            got = dot(parts, hot[step])
            block = jnp.broadcast_to(wanted // SUB - (first + start) // SUB, (rows, POS))
            if fresh:
                total = jnp.zeros((rows, POS), F32)
            else:
                total = jnp.concatenate(
                    [ordered[step * per + piece].astype(F32) for piece in range(per)], axis=1
                )
            for sub in range(pieces):
                total = jnp.where(block == sub, got[sub * rows:(sub + 1) * rows], total)
            for piece in range(per):
                ordered[step * per + piece] = total[:, piece * tile:(piece + 1) * tile].astype(BF16)
            return carry

        lax.fori_loop(0, order.shape[0], body, 0)

    def prepare_proj(height):
        loads[1 + 2 * height].wait()

        def body(step, carry):
            rows = pl.ds(step * 256, 256)
            high, low = split(proj_f[height, rows, :])
            proj_h[height, rows, :] = high
            proj_l[height, rows, :] = low
            return carry

        lax.fori_loop(0, half // 256, body, 0)

    def prepare_corr(height):
        loads[2 + 2 * height].wait()

        def body(step, carry):
            rows = pl.ds(step * 32, 32)
            high, low = split(corr_f[height, rows, :])
            corr_h[height, rows, :] = high
            corr_l[height, rows, :] = low
            return carry

        lax.fori_loop(0, corr.shape[1] // 32, body, 0)

    def prepare_near():
        loads[1 + 2 * heights].wait()

        def body(step, carry):
            for slot in range(slots):
                high, low = split(near_f[step, slot])
                near_hl[step, slot * tile:(slot + 1) * tile, :tile] = high
                near_hl[step, slot * tile:(slot + 1) * tile, tile:] = low
            return carry

        lax.fori_loop(0, tile_rows, body, 0)

    def prepare_coup():
        loads[2 + 2 * heights].wait()

        def body(step, carry):
            high, low = split(coup_f[step])
            coup_h[step] = high
            coup_l[step] = low
            return carry

        lax.fori_loop(0, heights, body, 0)

    loads[0].wait()
    place(mine, side * half, 0, half, True)
    for chunk in range(chunks):
        if chunk == 0:
            prepare_near()
        elif chunk == 1:
            prepare_proj(0)
            prepare_coup()
        elif chunk == 2:
            prepare_corr(0)
        elif chunk == 3:
            prepare_proj(1)
        arrivals[chunk].wait_recv()
        place(other, (1 - side) * half, chunk * SRC, SRC, False)

    for row in range(tile_rows):
        picked = []
        for slot in range(slots):
            live = jnp.where(slot < near_count[row], 1.0, 0.0).astype(F32)
            block = ordered[near_index[slot, row]]
            picked.append((block.astype(F32) * live).astype(BF16))
        four = dot(jnp.concatenate(picked, axis=1), near_hl[row])
        current[:, row * tile:(row + 1) * tile] = (
            four[:rhs_count, :tile] + (four[:rhs_count, tile:] + four[rhs_count:, :tile])
            + four[rhs_count:, tile:]
        )

    for height in range(heights):
        got = dot3(stacked(current[...]), proj_h[height], proj_l[height])
        part[height] = got.reshape(part.shape[1:])
        own = sib = None
        if height == 0:
            waits = []
            for rel in range(1, 4):
                there = rank0
                for bit in (1, 2):
                    if rel & bit:
                        there = flip(there, bit)
                waits.append(send(
                    part.at[0, pl.ds(2 * there, 2)], rs0.at[rel],
                    rs_send.at[0, rel], rs_recv.at[0, rel], plane(rel),
                ))
            prepare_corr(1)
            for wait in waits:
                wait.wait_recv()
            near_sum = part[0, pl.ds(2 * rank0, 2)] + rs0[1]
            far_sum = rs0[2] + rs0[3]
            stage0[0] = near_sum
            stage0[1] = far_sum
            stage0[2] = near_sum
            ag0[rank0, 0] = near_sum
            ag0[rank0, 1] = far_sum
            waits = []
            for rel in range(1, 4):
                first = 1 if rel & 2 else 0
                waits.append(send(
                    stage0.at[pl.ds(first, 2)], ag0.at[rank0],
                    ag_send.at[0, rel], ag_recv.at[0, rel], plane(rel),
                ))
            prepare_proj(2)
            for wait in waits:
                wait.wait_recv()
            own = ag0[:, 0].reshape(rhs_count, -1)
            sib = ag0[:, 1].reshape(rhs_count, -1)
        else:
            waits = []
            for rel in range(1, 8):
                waits.append(send(
                    part.at[height, rank_of(rel)], rs.at[height, rel],
                    rs_send.at[height, rel], rs_recv.at[height, rel], plane(rel),
                ))
            if height < 3:
                prepare_corr(height + 1)
            for wait in waits:
                wait.wait_recv()
            near_sum = (part[height, rank] + rs[height, 1]) + (rs[height, 2] + rs[height, 3])
            far_sum = (rs[height, 4] + rs[height, 5]) + (rs[height, 6] + rs[height, 7])
            swap = height == 1
            if height > 1:
                whole = near_sum + far_sum
                zsend[height] = whole
                waits = []
                for rel in range(1, 2 ** (height - 1)):
                    waits.append(send(
                        zsend.at[height], zrecv.at[height, rel],
                        z_send.at[height, rel], z_recv.at[height, rel], column_of(rel),
                    ))
                for wait in waits:
                    wait.wait_recv()
                if height == 2:
                    near_sum, far_sum = whole, zrecv[height, 1]
                else:
                    near_sum = whole + zrecv[height, 1]
                    far_sum = zrecv[height, 2] + zrecv[height, 3]
            stage[height, 0] = near_sum
            stage[height, 1] = far_sum
            stage[height, 2] = near_sum
            ag[height, rank, 0] = near_sum
            ag[height, rank, 1] = far_sum
            waits = []
            for rel in range(1, 8):
                first = 1 if swap and rel & 4 else 0
                waits.append(send(
                    stage.at[height, pl.ds(first, 2)], ag.at[height, rank],
                    ag_send.at[height, rel], ag_recv.at[height, rel], plane(rel),
                ))
            if height == 1:
                prepare_proj(3)
            for wait in waits:
                wait.wait_recv()
            own = ag[height, :, 0].reshape(rhs_count, -1)
            sib = ag[height, :, 1].reshape(rhs_count, -1)
        coeff = dot3(stacked(own), coup_h[height, 0], coup_l[height, 0])
        coeff = coeff + dot3(stacked(sib), coup_h[height, 1], coup_l[height, 1])
        change = dot3(stacked(coeff), corr_h[height], corr_l[height])
        if height < heights - 1:
            current[...] = current[...] - change
        else:
            out[...] = current[...] - change

    for copy in sends:
        copy.wait_send()


def local(
    charges, cluster_order, near_tiles, near_index, near_count, proj_basis, corr_basis, coupling
):
    rhs_count, half = charges.shape
    heights, _, rank = proj_basis.shape
    leaf_size = cluster_order.shape[0]
    tile_rows, slots, tile, _ = near_tiles.shape
    eighth = rhs_count // 8
    any_space = pl.BlockSpec(memory_space=pl.ANY)
    smem = pl.BlockSpec(memory_space=pltpu.SMEM)
    vmem = pl.BlockSpec(memory_space=pltpu.VMEM)
    dma = pltpu.SemaphoreType.DMA
    return pl.pallas_call(
        kernel,
        out_shape=jax.ShapeDtypeStruct((rhs_count, half), F32),
        in_specs=[smem, smem, vmem, any_space, any_space, any_space, any_space, any_space],
        out_specs=vmem,
        scratch_shapes=[
            pltpu.VMEM((rhs_count, half), F32),
            pltpu.VMEM((rhs_count, half), F32),
            pltpu.VMEM((leaf_size // POS, SUB, POS), BF16),
            pltpu.VMEM((leaf_size // tile, 2 * rhs_count, tile), BF16),
            pltpu.VMEM((tile_rows, slots, tile, tile), F32),
            pltpu.VMEM((tile_rows, slots * tile, 2 * tile), BF16),
            pltpu.VMEM((heights, half, rank), F32),
            pltpu.VMEM((heights, half, rank), BF16),
            pltpu.VMEM((heights, half, rank), BF16),
            pltpu.VMEM((heights, rank, half), F32),
            pltpu.VMEM((heights, rank, half), BF16),
            pltpu.VMEM((heights, rank, half), BF16),
            pltpu.VMEM((heights, 2, rank, rank), F32),
            pltpu.VMEM((heights, 2, rank, rank), BF16),
            pltpu.VMEM((heights, 2, rank, rank), BF16),
            pltpu.VMEM((rhs_count, half), F32),
            pltpu.VMEM((heights, 8, eighth, rank), F32),
            pltpu.VMEM((4, 2, eighth, rank), F32),
            pltpu.VMEM((3, 2, eighth, rank), F32),
            pltpu.VMEM((4, 2, 2, eighth, rank), F32),
            pltpu.VMEM((heights, 8, eighth, rank), F32),
            pltpu.VMEM((heights, 3, eighth, rank), F32),
            pltpu.VMEM((heights, 8, 2, eighth, rank), F32),
            pltpu.VMEM((heights, eighth, rank), F32),
            pltpu.VMEM((heights, 4, eighth, rank), F32),
            dma((3 + 2 * heights,)),
            dma((half // SRC,)),
            dma((half // SRC,)),
            dma((heights, 8)),
            dma((heights, 8)),
            dma((heights, 8)),
            dma((heights, 8)),
            dma((heights, 4)),
            dma((heights, 4)),
        ],
        compiler_params=pltpu.CompilerParams(
            collective_id=0, has_side_effects=True, vmem_limit_bytes=60 * 2**20
        ),
        name="solve",
    )(
        near_index.T,
        near_count,
        cluster_order.reshape(leaf_size // POS, 1, POS),
        charges,
        near_tiles,
        proj_basis,
        corr_basis,
        coupling[0],
    )


def solution(mesh):
    return jax.shard_map(
        local,
        mesh=mesh,
        in_specs=(
            P(None, ("level", "leaf", "rhs")),
            P(("level", "leaf")),
            P(("level", "leaf", "rhs"), None, None, None),
            P(("level", "leaf", "rhs"), None),
            P(("level", "leaf", "rhs")),
            P(None, ("level", "leaf", "rhs"), None),
            P(None, None, ("level", "leaf", "rhs")),
            P(("level", "leaf"), None, None, None, None),
        ),
        out_specs=P(None, ("level", "leaf", "rhs")),
        check_vma=False,
    )
```

```python
import jax
import jax.numpy as jnp
from jax import lax
from jax.experimental import pallas as pl
from jax.experimental.pallas import tpu as pltpu
from jax.sharding import PartitionSpec as P

F32 = jnp.float32
BF16 = jnp.bfloat16
MESH = pl.DeviceIdType.MESH
POS = 512
SRC = 512
SUB = 256


def flip(index, bit):
    return index + bit - 2 * bit * ((index // bit) % 2)


def split(values):
    high = values.astype(BF16)
    low = (values - high.astype(F32)).astype(BF16)
    return high, low


def stacked(values):
    return jnp.concatenate(split(values), axis=0)


def dot(left, right):
    return jnp.dot(left, right, preferred_element_type=F32)


def dot3(left_hl, right_high, right_low):
    rows = left_hl.shape[0] // 2
    both = dot(left_hl, right_high)
    return both[:rows] + both[rows:] + dot(left_hl[:rows], right_low)


def kernel(
    near_index, near_count, order, charges, near, proj, corr, coup, out,
    mine, other, hot, ordered, near_f, near_hl, proj_f, proj_h, proj_l, corr_f, corr_h, corr_l,
    coup_f, coup_h, coup_l, gram_h, gram_l, current, cur_hl, coeffs, part, rs0, stage0, ag0, rs, stage, ag, zsend, zrecv,
    load_sem, ex_send, ex_recv, rs_send, rs_recv, ag_send, ag_recv, z_send, z_recv,
):
    heights = proj.shape[0]
    rhs_count, half = charges.shape
    level, leaf, side = lax.axis_index("level"), lax.axis_index("leaf"), lax.axis_index("rhs")
    core, column = leaf % 2, leaf // 2
    rank = side + 2 * core + 4 * column
    rank0 = side + 2 * core

    def rank_of(rel):
        number = rank
        for bit in (1, 2, 4):
            if rel & bit:
                number = flip(number, bit)
        return number

    def plane(rel, over=0):
        where, there = leaf, side
        if rel & 1:
            there = 1 - side
        if rel & 2:
            where = flip(where, 1)
        if rel & 4:
            where = flip(where, 2)
        return {"level": flip(level, 1) if over else level, "leaf": where, "rhs": there}

    def column_of(rel):
        number = level
        for bit in (1, 2):
            if rel & bit:
                number = flip(number, bit)
        return {"level": number, "leaf": leaf, "rhs": side}

    loads = [pltpu.make_async_copy(charges, mine, load_sem.at[0])]
    for height in range(heights):
        loads.append(pltpu.make_async_copy(proj.at[height], proj_f.at[height], load_sem.at[1 + 2 * height]))
        loads.append(pltpu.make_async_copy(corr.at[height], corr_f.at[height], load_sem.at[2 + 2 * height]))
    loads.append(pltpu.make_async_copy(near, near_f, load_sem.at[1 + 2 * heights]))
    loads.append(pltpu.make_async_copy(coup, coup_f, load_sem.at[2 + 2 * heights]))
    for load in [loads[0], loads[1 + 2 * heights], loads[1], loads[2 + 2 * heights]] + loads[2:1 + 2 * heights]:
        load.start()

    barrier = pltpu.get_barrier_semaphore()
    for rel in range(1, 8):
        pl.semaphore_signal(barrier, inc=1, device_id=plane(rel), device_id_type=MESH)
    for rel in range(1, 4):
        pl.semaphore_signal(barrier, inc=1, device_id=column_of(rel), device_id_type=MESH)
    for rel in range(1, 8):
        pl.semaphore_signal(barrier, inc=1, device_id=plane(rel, 1), device_id_type=MESH)
    pl.semaphore_wait(barrier, 17)

    sends = []

    def send(src, dst, send_sem, recv_sem, device):
        copy = pltpu.make_async_remote_copy(
            src_ref=src, dst_ref=dst, send_sem=send_sem, recv_sem=recv_sem,
            device_id=device, device_id_type=MESH,
        )
        copy.start()
        sends.append(copy)
        return copy

    chunks = half // SRC
    arrivals = []
    for chunk in range(chunks):
        cols = pl.ds(chunk * SRC, SRC)
        arrivals.append(send(
            charges.at[:, cols], other.at[:, cols], ex_send.at[chunk], ex_recv.at[chunk], plane(1)
        ))

    rows_of = lax.broadcasted_iota(jnp.int32, (SUB, POS), 0)
    tile_rows, slots, tile = near.shape[0], near.shape[1], near.shape[2]
    per = POS // tile

    def place(source, first, start, width, fresh):
        pieces = width // SUB
        parts = jnp.concatenate(
            [stacked(source[:, start + sub * SUB:start + (sub + 1) * SUB]) for sub in range(pieces)], axis=0
        )
        rows = 2 * rhs_count

        def body(step, carry):
            wanted = order[step]
            if fresh:
                hot[step] = jnp.where(rows_of == wanted % SUB, 1.0, 0.0).astype(BF16)
            got = dot(parts, hot[step])
            block = jnp.broadcast_to(wanted // SUB - (first + start) // SUB, (rows, POS))
            if fresh:
                total = jnp.zeros((rows, POS), F32)
            else:
                total = jnp.concatenate(
                    [ordered[step * per + piece].astype(F32) for piece in range(per)], axis=1
                )
            for sub in range(pieces):
                total = jnp.where(block == sub, got[sub * rows:(sub + 1) * rows], total)
            for piece in range(per):
                ordered[step * per + piece] = total[:, piece * tile:(piece + 1) * tile].astype(BF16)
            return carry

        lax.fori_loop(0, order.shape[0], body, 0)

    def prepare_proj(height):
        loads[1 + 2 * height].wait()

        def body(step, carry):
            rows = pl.ds(step * 256, 256)
            high, low = split(proj_f[height, rows, :])
            proj_h[height, rows, :] = high
            proj_l[height, rows, :] = low
            return carry

        lax.fori_loop(0, half // 256, body, 0)

    def prepare_corr(height):
        loads[2 + 2 * height].wait()

        def body(step, carry):
            rows = pl.ds(step * 32, 32)
            high, low = split(corr_f[height, rows, :])
            corr_h[height, rows, :] = high
            corr_l[height, rows, :] = low
            return carry

        lax.fori_loop(0, corr.shape[1] // 32, body, 0)

    def prepare_near():
        loads[1 + 2 * heights].wait()

        def body(step, carry):
            for slot in range(slots):
                high, low = split(near_f[step, slot])
                near_hl[step, slot * tile:(slot + 1) * tile, :tile] = high
                near_hl[step, slot * tile:(slot + 1) * tile, tile:] = low
            return carry

        lax.fori_loop(0, tile_rows, body, 0)

    def prepare_coup():
        loads[2 + 2 * heights].wait()

        def body(step, carry):
            high, low = split(coup_f[step])
            coup_h[step] = high
            coup_l[step] = low
            return carry

        lax.fori_loop(0, heights, body, 0)

    def gram(low, high):
        left = jnp.concatenate([corr_h[low], corr_l[low]], axis=0)
        top, bottom = split(dot3(left, proj_h[high], proj_l[high]))
        gram_h[low, high] = top
        gram_l[low, high] = bottom

    def project(height):
        got = dot3(cur_hl[...], proj_h[height], proj_l[height])
        part[height] = got.reshape(part.shape[1:])

    def lower(low, high):
        got = dot3(coeffs[low], gram_h[low, high], gram_l[low, high])
        part[high] = part[high] - got.reshape(part.shape[1:])

    def correct(height):
        current[...] = current[...] - dot3(coeffs[height], corr_h[height], corr_l[height])

    loads[0].wait()
    place(mine, side * half, 0, half, True)
    for chunk in range(chunks):
        if chunk == 0:
            prepare_near()
        elif chunk == 1:
            prepare_proj(0)
            prepare_coup()
        elif chunk == 2:
            prepare_corr(0)
            prepare_proj(1)
        elif chunk == 3:
            gram(0, 1)
            prepare_proj(2)
        arrivals[chunk].wait_recv()
        place(other, (1 - side) * half, chunk * SRC, SRC, False)

    for row in range(tile_rows):
        picked = []
        for slot in range(slots):
            live = jnp.where(slot < near_count[row], 1.0, 0.0).astype(F32)
            block = ordered[near_index[slot, row]]
            picked.append((block.astype(F32) * live).astype(BF16))
        four = dot(jnp.concatenate(picked, axis=1), near_hl[row])
        current[:, row * tile:(row + 1) * tile] = (
            four[:rhs_count, :tile] + (four[:rhs_count, tile:] + four[rhs_count:, :tile])
            + four[rhs_count:, tile:]
        )

    cur_hl[...] = stacked(current[...])
    project(0)

    for height in range(heights):
        own = sib = None
        if height == 0:
            waits = []
            for rel in range(1, 4):
                there = rank0
                for bit in (1, 2):
                    if rel & bit:
                        there = flip(there, bit)
                waits.append(send(
                    part.at[0, pl.ds(2 * there, 2)], rs0.at[rel],
                    rs_send.at[0, rel], rs_recv.at[0, rel], plane(rel),
                ))
            project(1)
            prepare_corr(1)
            for wait in waits:
                wait.wait_recv()
            near_sum = part[0, pl.ds(2 * rank0, 2)] + rs0[1]
            far_sum = rs0[2] + rs0[3]
            stage0[0] = near_sum
            stage0[1] = far_sum
            stage0[2] = near_sum
            ag0[rank0, 0] = near_sum
            ag0[rank0, 1] = far_sum
            waits = []
            for rel in range(1, 4):
                first = 1 if rel & 2 else 0
                waits.append(send(
                    stage0.at[pl.ds(first, 2)], ag0.at[rank0],
                    ag_send.at[0, rel], ag_recv.at[0, rel], plane(rel),
                ))
            project(2)
            gram(0, 2)
            for wait in waits:
                wait.wait_recv()
            own = ag0[:, 0].reshape(rhs_count, -1)
            sib = ag0[:, 1].reshape(rhs_count, -1)
        else:
            waits = []
            for rel in range(1, 8):
                waits.append(send(
                    part.at[height, rank_of(rel)], rs.at[height, rel],
                    rs_send.at[height, rel], rs_recv.at[height, rel], plane(rel),
                ))
            if height == 1:
                gram(1, 2)
                lower(0, 2)
                prepare_proj(3)
            elif height == 2:
                gram(1, 3)
                lower(0, 3)
                gram(2, 3)
            else:
                correct(1)
                correct(2)
            for wait in waits:
                wait.wait_recv()
            near_sum = (part[height, rank] + rs[height, 1]) + (rs[height, 2] + rs[height, 3])
            far_sum = (rs[height, 4] + rs[height, 5]) + (rs[height, 6] + rs[height, 7])
            swap = height == 1
            waits = []
            if height == 2:
                whole = near_sum + far_sum
                zsend[height] = whole
                ag[height, rank, 0] = whole
                for rel in range(8):
                    waits.append(send(
                        zsend.at[height], ag.at[height, rank, 1],
                        z_send.at[height, rel], z_recv.at[height, rel], plane(rel, 1),
                    ))
                for rel in range(1, 8):
                    waits.append(send(
                        zsend.at[height], ag.at[height, rank, 0],
                        ag_send.at[height, rel], ag_recv.at[height, rel], plane(rel),
                    ))
            else:
                if height == 3:
                    whole = near_sum + far_sum
                    zsend[height] = whole
                    crossings = []
                    for rel in range(1, 4):
                        crossings.append(send(
                            zsend.at[height], zrecv.at[height, rel],
                            z_send.at[height, rel], z_recv.at[height, rel], column_of(rel),
                        ))
                    for wait in crossings:
                        wait.wait_recv()
                    near_sum = whole + zrecv[height, 1]
                    far_sum = zrecv[height, 2] + zrecv[height, 3]
                stage[height, 0] = near_sum
                stage[height, 1] = far_sum
                stage[height, 2] = near_sum
                ag[height, rank, 0] = near_sum
                ag[height, rank, 1] = far_sum
                for rel in range(1, 8):
                    first = 1 if swap and rel & 4 else 0
                    waits.append(send(
                        stage.at[height, pl.ds(first, 2)], ag.at[height, rank],
                        ag_send.at[height, rel], ag_recv.at[height, rel], plane(rel),
                    ))
            if height == 1:
                project(3)
                prepare_corr(2)
                gram(0, 3)
            elif height == 2:
                lower(1, 3)
                prepare_corr(3)
                correct(0)
            for wait in waits:
                wait.wait_recv()
            own = ag[height, :, 0].reshape(rhs_count, -1)
            sib = ag[height, :, 1].reshape(rhs_count, -1)
        coeff = dot3(stacked(own), coup_h[height, 0], coup_l[height, 0])
        coeff = coeff + dot3(stacked(sib), coup_h[height, 1], coup_l[height, 1])
        coeffs[height] = stacked(coeff)
        if height < heights - 1:
            lower(height, height + 1)
        else:
            out[...] = current[...] - dot3(coeffs[height], corr_h[height], corr_l[height])

    for copy in sends:
        copy.wait_send()


def local(
    charges, cluster_order, near_tiles, near_index, near_count, proj_basis, corr_basis, coupling
):
    rhs_count, half = charges.shape
    heights, _, rank = proj_basis.shape
    leaf_size = cluster_order.shape[0]
    tile_rows, slots, tile, _ = near_tiles.shape
    eighth = rhs_count // 8
    any_space = pl.BlockSpec(memory_space=pl.ANY)
    smem = pl.BlockSpec(memory_space=pltpu.SMEM)
    vmem = pl.BlockSpec(memory_space=pltpu.VMEM)
    dma = pltpu.SemaphoreType.DMA
    return pl.pallas_call(
        kernel,
        out_shape=jax.ShapeDtypeStruct((rhs_count, half), F32),
        in_specs=[smem, smem, vmem, any_space, any_space, any_space, any_space, any_space],
        out_specs=vmem,
        scratch_shapes=[
            pltpu.VMEM((rhs_count, half), F32),
            pltpu.VMEM((rhs_count, half), F32),
            pltpu.VMEM((leaf_size // POS, SUB, POS), BF16),
            pltpu.VMEM((leaf_size // tile, 2 * rhs_count, tile), BF16),
            pltpu.VMEM((tile_rows, slots, tile, tile), F32),
            pltpu.VMEM((tile_rows, slots * tile, 2 * tile), BF16),
            pltpu.VMEM((heights, half, rank), F32),
            pltpu.VMEM((heights, half, rank), BF16),
            pltpu.VMEM((heights, half, rank), BF16),
            pltpu.VMEM((heights, rank, half), F32),
            pltpu.VMEM((heights, rank, half), BF16),
            pltpu.VMEM((heights, rank, half), BF16),
            pltpu.VMEM((heights, 2, rank, rank), F32),
            pltpu.VMEM((heights, 2, rank, rank), BF16),
            pltpu.VMEM((heights, 2, rank, rank), BF16),
            pltpu.VMEM((heights, heights, rank, rank), BF16),
            pltpu.VMEM((heights, heights, rank, rank), BF16),
            pltpu.VMEM((rhs_count, half), F32),
            pltpu.VMEM((2 * rhs_count, half), BF16),
            pltpu.VMEM((heights, 2 * rhs_count, rank), BF16),
            pltpu.VMEM((heights, 8, eighth, rank), F32),
            pltpu.VMEM((4, 2, eighth, rank), F32),
            pltpu.VMEM((3, 2, eighth, rank), F32),
            pltpu.VMEM((4, 2, 2, eighth, rank), F32),
            pltpu.VMEM((heights, 8, eighth, rank), F32),
            pltpu.VMEM((heights, 3, eighth, rank), F32),
            pltpu.VMEM((heights, 8, 2, eighth, rank), F32),
            pltpu.VMEM((heights, eighth, rank), F32),
            pltpu.VMEM((heights, 4, eighth, rank), F32),
            dma((3 + 2 * heights,)),
            dma((half // SRC,)),
            dma((half // SRC,)),
            dma((heights, 8)),
            dma((heights, 8)),
            dma((heights, 8)),
            dma((heights, 8)),
            dma((heights, 8)),
            dma((heights, 8)),
        ],
        compiler_params=pltpu.CompilerParams(
            collective_id=0, has_side_effects=True, vmem_limit_bytes=60 * 2**20
        ),
        name="solve",
    )(
        near_index.T,
        near_count,
        cluster_order.reshape(leaf_size // POS, 1, POS),
        charges,
        near_tiles,
        proj_basis,
        corr_basis,
        coupling[0],
    )


def solution(mesh):
    return jax.shard_map(
        local,
        mesh=mesh,
        in_specs=(
            P(None, ("level", "leaf", "rhs")),
            P(("level", "leaf")),
            P(("level", "leaf", "rhs"), None, None, None),
            P(("level", "leaf", "rhs"), None),
            P(("level", "leaf", "rhs")),
            P(None, ("level", "leaf", "rhs"), None),
            P(None, None, ("level", "leaf", "rhs")),
            P(("level", "leaf"), None, None, None, None),
        ),
        out_specs=P(None, ("level", "leaf", "rhs")),
        check_vma=False,
    )
```

```python
import jax
import jax.numpy as jnp
from jax import lax
from jax.experimental import pallas as pl
from jax.experimental.pallas import tpu as pltpu
from jax.sharding import PartitionSpec as P

F32 = jnp.float32
BF16 = jnp.bfloat16
MESH = pl.DeviceIdType.MESH
POS = 512
SRC = 512
SUB = 256


def flip(index, bit):
    return index + bit - 2 * bit * ((index // bit) % 2)


def split(values):
    high = values.astype(BF16)
    low = (values - high.astype(F32)).astype(BF16)
    return high, low


def stacked(values):
    return jnp.concatenate(split(values), axis=0)


def dot(left, right):
    return jnp.dot(left, right, preferred_element_type=F32)


def dot3(left_hl, right_high, right_low):
    rows = left_hl.shape[0] // 2
    both = dot(left_hl, right_high)
    return both[:rows] + both[rows:] + dot(left_hl[:rows], right_low)


def kernel(
    near_index, near_count, order, charges, near, proj, corr, coup, out,
    mine, other, hot, ordered, near_f, near_hl, proj_f, proj_h, proj_l, corr_f, corr_h, corr_l,
    coup_f, coup_h, coup_l, gram_h, gram_l, current, cur_hl, coeffs, part, rs0, stage0, ag0, rs, stage, ag, zsend, zrecv,
    load_sem, ex_send, ex_recv, rs_send, rs_recv, ag_send, ag_recv, z_send, z_recv,
):
    heights = proj.shape[0]
    rhs_count, half = charges.shape
    level, leaf, side = lax.axis_index("level"), lax.axis_index("leaf"), lax.axis_index("rhs")
    core, column = leaf % 2, leaf // 2
    rank = side + 2 * core + 4 * column
    rank0 = side + 2 * core

    def rank_of(rel):
        number = rank
        for bit in (1, 2, 4):
            if rel & bit:
                number = flip(number, bit)
        return number

    def plane(rel, over=0):
        where, there = leaf, side
        if rel & 1:
            there = 1 - side
        if rel & 2:
            where = flip(where, 1)
        if rel & 4:
            where = flip(where, 2)
        return {"level": flip(level, 1) if over else level, "leaf": where, "rhs": there}

    def column_of(rel):
        number = level
        for bit in (1, 2):
            if rel & bit:
                number = flip(number, bit)
        return {"level": number, "leaf": leaf, "rhs": side}

    loads = [pltpu.make_async_copy(charges, mine, load_sem.at[0])]
    for height in range(heights):
        loads.append(pltpu.make_async_copy(proj.at[height], proj_f.at[height], load_sem.at[1 + 2 * height]))
        loads.append(pltpu.make_async_copy(corr.at[height], corr_f.at[height], load_sem.at[2 + 2 * height]))
    loads.append(pltpu.make_async_copy(near, near_f, load_sem.at[1 + 2 * heights]))
    loads.append(pltpu.make_async_copy(coup, coup_f, load_sem.at[2 + 2 * heights]))
    for load in [loads[0], loads[1 + 2 * heights], loads[1]]:
        load.start()

    barrier = pltpu.get_barrier_semaphore()
    for rel in range(1, 8):
        pl.semaphore_signal(barrier, inc=1, device_id=plane(rel), device_id_type=MESH)
    for rel in range(1, 4):
        pl.semaphore_signal(barrier, inc=1, device_id=column_of(rel), device_id_type=MESH)
    for rel in range(1, 8):
        pl.semaphore_signal(barrier, inc=1, device_id=plane(rel, 1), device_id_type=MESH)
    pl.semaphore_wait(barrier, 17)

    sends = []

    def send(src, dst, send_sem, recv_sem, device):
        copy = pltpu.make_async_remote_copy(
            src_ref=src, dst_ref=dst, send_sem=send_sem, recv_sem=recv_sem,
            device_id=device, device_id_type=MESH,
        )
        copy.start()
        sends.append(copy)
        return copy

    chunks = half // SRC
    arrivals = []
    for chunk in range(chunks):
        cols = pl.ds(chunk * SRC, SRC)
        arrivals.append(send(
            charges.at[:, cols], other.at[:, cols], ex_send.at[chunk], ex_recv.at[chunk], plane(1)
        ))

    for load in [loads[2 + 2 * heights]] + loads[2:1 + 2 * heights]:
        load.start()

    rows_of = lax.broadcasted_iota(jnp.int32, (SUB, POS), 0)
    tile_rows, slots, tile = near.shape[0], near.shape[1], near.shape[2]
    per = POS // tile

    def place(source, first, start, width, fresh):
        pieces = width // SUB
        parts = jnp.concatenate(
            [stacked(source[:, start + sub * SUB:start + (sub + 1) * SUB]) for sub in range(pieces)], axis=0
        )
        rows = 2 * rhs_count

        def body(step, carry):
            wanted = order[step]
            if fresh:
                hot[step] = jnp.where(rows_of == wanted % SUB, 1.0, 0.0).astype(BF16)
            got = dot(parts, hot[step])
            block = jnp.broadcast_to(wanted // SUB - (first + start) // SUB, (rows, POS))
            if fresh:
                total = jnp.zeros((rows, POS), F32)
            else:
                total = jnp.concatenate(
                    [ordered[step * per + piece].astype(F32) for piece in range(per)], axis=1
                )
            for sub in range(pieces):
                total = jnp.where(block == sub, got[sub * rows:(sub + 1) * rows], total)
            for piece in range(per):
                ordered[step * per + piece] = total[:, piece * tile:(piece + 1) * tile].astype(BF16)
            return carry

        lax.fori_loop(0, order.shape[0], body, 0)

    def prepare_proj(height):
        loads[1 + 2 * height].wait()

        def body(step, carry):
            rows = pl.ds(step * 256, 256)
            high, low = split(proj_f[height, rows, :])
            proj_h[height, rows, :] = high
            proj_l[height, rows, :] = low
            return carry

        lax.fori_loop(0, half // 256, body, 0)

    def prepare_corr(height):
        loads[2 + 2 * height].wait()

        def body(step, carry):
            rows = pl.ds(step * 32, 32)
            high, low = split(corr_f[height, rows, :])
            corr_h[height, rows, :] = high
            corr_l[height, rows, :] = low
            return carry

        lax.fori_loop(0, corr.shape[1] // 32, body, 0)

    def prepare_near():
        loads[1 + 2 * heights].wait()

        def body(step, carry):
            for slot in range(slots):
                high, low = split(near_f[step, slot])
                near_hl[step, slot * tile:(slot + 1) * tile, :tile] = high
                near_hl[step, slot * tile:(slot + 1) * tile, tile:] = low
            return carry

        lax.fori_loop(0, tile_rows, body, 0)

    def prepare_coup():
        loads[2 + 2 * heights].wait()

        def body(step, carry):
            high, low = split(coup_f[step])
            coup_h[step] = high
            coup_l[step] = low
            return carry

        lax.fori_loop(0, heights, body, 0)

    def gram(low, high):
        left = jnp.concatenate([corr_h[low], corr_l[low]], axis=0)
        top, bottom = split(dot3(left, proj_h[high], proj_l[high]))
        gram_h[low] = top
        gram_l[low] = bottom

    def project(height):
        got = dot3(cur_hl[...], proj_h[height], proj_l[height])
        part[height] = got.reshape(part.shape[1:])

    def lower(low, high):
        got = dot3(coeffs[low], gram_h[low], gram_l[low])
        part[high] = part[high] - got.reshape(part.shape[1:])

    def correct(height):
        left = current[...] - dot3(coeffs[height], corr_h[height], corr_l[height])
        current[...] = left
        if height < heights - 2:
            cur_hl[...] = stacked(left)

    loads[0].wait()
    place(mine, side * half, 0, half, True)
    for chunk in range(chunks):
        if chunk == 0:
            prepare_near()
        elif chunk == 1:
            prepare_proj(0)
            prepare_coup()
        elif chunk == 2:
            prepare_corr(0)
            prepare_proj(1)
        elif chunk == 3:
            gram(0, 1)
            prepare_proj(2)
        arrivals[chunk].wait_recv()
        place(other, (1 - side) * half, chunk * SRC, SRC, False)

    for row in range(tile_rows):
        picked = []
        for slot in range(slots):
            live = jnp.where(slot < near_count[row], 1.0, 0.0).astype(F32)
            block = ordered[near_index[slot, row]]
            picked.append((block.astype(F32) * live).astype(BF16))
        four = dot(jnp.concatenate(picked, axis=1), near_hl[row])
        current[:, row * tile:(row + 1) * tile] = (
            four[:rhs_count, :tile] + (four[:rhs_count, tile:] + four[rhs_count:, :tile])
            + four[rhs_count:, tile:]
        )

    cur_hl[...] = stacked(current[...])
    project(0)

    for height in range(heights):
        own = sib = None
        if height == 0:
            waits = []
            for rel in range(1, 4):
                there = rank0
                for bit in (1, 2):
                    if rel & bit:
                        there = flip(there, bit)
                waits.append(send(
                    part.at[0, pl.ds(2 * there, 2)], rs0.at[rel],
                    rs_send.at[0, rel], rs_recv.at[0, rel], plane(rel),
                ))
            project(1)
            prepare_corr(1)
            for wait in waits:
                wait.wait_recv()
            near_sum = part[0, pl.ds(2 * rank0, 2)] + rs0[1]
            far_sum = rs0[2] + rs0[3]
            stage0[0] = near_sum
            stage0[1] = far_sum
            stage0[2] = near_sum
            ag0[rank0, 0] = near_sum
            ag0[rank0, 1] = far_sum
            waits = []
            for rel in range(1, 4):
                first = 1 if rel & 2 else 0
                waits.append(send(
                    stage0.at[pl.ds(first, 2)], ag0.at[rank0],
                    ag_send.at[0, rel], ag_recv.at[0, rel], plane(rel),
                ))
            gram(1, 2)
            for wait in waits:
                wait.wait_recv()
            own = ag0[:, 0].reshape(rhs_count, -1)
            sib = ag0[:, 1].reshape(rhs_count, -1)
        else:
            waits = []
            for rel in range(1, 8):
                waits.append(send(
                    part.at[height, rank_of(rel)], rs.at[height, rel],
                    rs_send.at[height, rel], rs_recv.at[height, rel], plane(rel),
                ))
            if height == 1:
                correct(0)
                prepare_proj(3)
            elif height == 2:
                correct(1)
                gram(2, 3)
            else:
                correct(2)
            for wait in waits:
                wait.wait_recv()
            near_sum = (part[height, rank] + rs[height, 1]) + (rs[height, 2] + rs[height, 3])
            far_sum = (rs[height, 4] + rs[height, 5]) + (rs[height, 6] + rs[height, 7])
            swap = height == 1
            waits = []
            if height == 2:
                whole = near_sum + far_sum
                zsend[height] = whole
                ag[height, rank, 0] = whole
                for rel in range(8):
                    waits.append(send(
                        zsend.at[height], ag.at[height, rank, 1],
                        z_send.at[height, rel], z_recv.at[height, rel], plane(rel, 1),
                    ))
                for rel in range(1, 8):
                    waits.append(send(
                        zsend.at[height], ag.at[height, rank, 0],
                        ag_send.at[height, rel], ag_recv.at[height, rel], plane(rel),
                    ))
            else:
                if height == 3:
                    whole = near_sum + far_sum
                    zsend[height] = whole
                    crossings = []
                    for rel in range(1, 4):
                        crossings.append(send(
                            zsend.at[height], zrecv.at[height, rel],
                            z_send.at[height, rel], z_recv.at[height, rel], column_of(rel),
                        ))
                    for wait in crossings:
                        wait.wait_recv()
                    near_sum = whole + zrecv[height, 1]
                    far_sum = zrecv[height, 2] + zrecv[height, 3]
                stage[height, 0] = near_sum
                stage[height, 1] = far_sum
                stage[height, 2] = near_sum
                ag[height, rank, 0] = near_sum
                ag[height, rank, 1] = far_sum
                for rel in range(1, 8):
                    first = 1 if swap and rel & 4 else 0
                    waits.append(send(
                        stage.at[height, pl.ds(first, 2)], ag.at[height, rank],
                        ag_send.at[height, rel], ag_recv.at[height, rel], plane(rel),
                    ))
            if height == 1:
                project(2)
                prepare_corr(2)
            elif height == 2:
                project(3)
                prepare_corr(3)
            for wait in waits:
                wait.wait_recv()
            own = ag[height, :, 0].reshape(rhs_count, -1)
            sib = ag[height, :, 1].reshape(rhs_count, -1)
        coeff = dot3(stacked(own), coup_h[height, 0], coup_l[height, 0])
        coeff = coeff + dot3(stacked(sib), coup_h[height, 1], coup_l[height, 1])
        coeffs[height] = stacked(coeff)
        if height < heights - 1:
            lower(height, height + 1)
        else:
            out[...] = current[...] - dot3(coeffs[height], corr_h[height], corr_l[height])

    for copy in sends:
        copy.wait_send()


def local(
    charges, cluster_order, near_tiles, near_index, near_count, proj_basis, corr_basis, coupling
):
    rhs_count, half = charges.shape
    heights, _, rank = proj_basis.shape
    leaf_size = cluster_order.shape[0]
    tile_rows, slots, tile, _ = near_tiles.shape
    eighth = rhs_count // 8
    any_space = pl.BlockSpec(memory_space=pl.ANY)
    smem = pl.BlockSpec(memory_space=pltpu.SMEM)
    vmem = pl.BlockSpec(memory_space=pltpu.VMEM)
    dma = pltpu.SemaphoreType.DMA
    return pl.pallas_call(
        kernel,
        out_shape=jax.ShapeDtypeStruct((rhs_count, half), F32),
        in_specs=[smem, smem, vmem, any_space, any_space, any_space, any_space, any_space],
        out_specs=vmem,
        scratch_shapes=[
            pltpu.VMEM((rhs_count, half), F32),
            pltpu.VMEM((rhs_count, half), F32),
            pltpu.VMEM((leaf_size // POS, SUB, POS), BF16),
            pltpu.VMEM((leaf_size // tile, 2 * rhs_count, tile), BF16),
            pltpu.VMEM((tile_rows, slots, tile, tile), F32),
            pltpu.VMEM((tile_rows, slots * tile, 2 * tile), BF16),
            pltpu.VMEM((heights, half, rank), F32),
            pltpu.VMEM((heights, half, rank), BF16),
            pltpu.VMEM((heights, half, rank), BF16),
            pltpu.VMEM((heights, rank, half), F32),
            pltpu.VMEM((heights, rank, half), BF16),
            pltpu.VMEM((heights, rank, half), BF16),
            pltpu.VMEM((heights, 2, rank, rank), F32),
            pltpu.VMEM((heights, 2, rank, rank), BF16),
            pltpu.VMEM((heights, 2, rank, rank), BF16),
            pltpu.VMEM((heights, rank, rank), BF16),
            pltpu.VMEM((heights, rank, rank), BF16),
            pltpu.VMEM((rhs_count, half), F32),
            pltpu.VMEM((2 * rhs_count, half), BF16),
            pltpu.VMEM((heights, 2 * rhs_count, rank), BF16),
            pltpu.VMEM((heights, 8, eighth, rank), F32),
            pltpu.VMEM((4, 2, eighth, rank), F32),
            pltpu.VMEM((3, 2, eighth, rank), F32),
            pltpu.VMEM((4, 2, 2, eighth, rank), F32),
            pltpu.VMEM((heights, 8, eighth, rank), F32),
            pltpu.VMEM((heights, 3, eighth, rank), F32),
            pltpu.VMEM((heights, 8, 2, eighth, rank), F32),
            pltpu.VMEM((heights, eighth, rank), F32),
            pltpu.VMEM((heights, 4, eighth, rank), F32),
            dma((3 + 2 * heights,)),
            dma((half // SRC,)),
            dma((half // SRC,)),
            dma((heights, 8)),
            dma((heights, 8)),
            dma((heights, 8)),
            dma((heights, 8)),
            dma((heights, 8)),
            dma((heights, 8)),
        ],
        compiler_params=pltpu.CompilerParams(
            collective_id=0, has_side_effects=True, vmem_limit_bytes=60 * 2**20
        ),
        name="solve",
    )(
        near_index.T,
        near_count,
        cluster_order.reshape(leaf_size // POS, 1, POS),
        charges,
        near_tiles,
        proj_basis,
        corr_basis,
        coupling[0],
    )


def solution(mesh):
    return jax.shard_map(
        local,
        mesh=mesh,
        in_specs=(
            P(None, ("level", "leaf", "rhs")),
            P(("level", "leaf")),
            P(("level", "leaf", "rhs"), None, None, None),
            P(("level", "leaf", "rhs"), None),
            P(("level", "leaf", "rhs")),
            P(None, ("level", "leaf", "rhs"), None),
            P(None, None, ("level", "leaf", "rhs")),
            P(("level", "leaf"), None, None, None, None),
        ),
        out_specs=P(None, ("level", "leaf", "rhs")),
        check_vma=False,
    )
```
